32 devices in a mesh: group: 2 (over y), expert: 4 (over z), dp: 2 (over x), tensor: 2 (over core).
Axes of the slice: x: 2, y: 2, z: 4, core: 2. Of those that a mesh axis runs over, the one named last changes fastest.
Arguments:
- incoming_activation_vectors: bfloat16 [1024, 3072], P(('group', 'expert', 'dp'), 'tensor'), parts along dimension 0, may hold values from -6 to 6
- routed_specialist_pairs: int32 [1024, 2], P(('group', 'expert', 'dp')), parts along dimension 0, may hold values from 0 to 3, as said below
- routing_shares: float32 [1024, 2], P(('group', 'expert', 'dp')), parts along dimension 0, may hold values from 0.2 to 1
- popular_specialist_flags: int32 [8], P('group'), parts along dimension 0, may hold values from 0 to 1, as said below
- group_quotas: int32 [8], P('group'), parts along dimension 0, may hold values from 8 to 16
- gating_weight_stack: bfloat16 [3072, 32768], P('dp', ('expert', 'tensor')), may hold values from -0.109375 to 0.109375
- widen_weight_stack: bfloat16 [3072, 32768], P('dp', ('expert', 'tensor')), may hold values from -0.109375 to 0.109375
- contract_weight_stack: bfloat16 [32768, 3072], P(('expert', 'tensor'), 'dp'), may hold values from -0.0625 to 0.0625
Outputs:
- mixed: bfloat16 [1024, 3072], P(('group', 'expert', 'dp'), 'tensor'), parts along dimension 0
The draws below stay inside these ranges and needn't reach their ends.
There are 2 independent parts, one for each index of `group`. The reference program is written for one: setup_inputs(seed, part) draws one part's arguments, and reference() takes and returns one part's arrays. A program takes and returns all parts, laid end to end along the dimension named above; an argument that names none is the same for every part. Nothing has to cross between parts.
Inputs may be any that keep to these rules, and one draw needn't show every extreme that they name: `routed_specialist_pairs`: each token names two different experts. Every expert with popular_specialist_flags 1 is named by at least 32 tokens of every aligned block of 64 tokens. `popular_specialist_flags`: one or two experts have the value 1.
All inputs are finite; a program needn't handle non-finite values.
Results may differ from the reference program's by a relative error of at most 0.0058.
Values may be sent and summed in bfloat16 or wider, within the bound.
A program may use at most 256 MiB of HBM per device.

```python
import jax
import jax.numpy as jnp
from jax import lax

D = 3072
F = 8192
EXPERTS = 4
TOK = 64
GROUP_QUOTA = 32
TOKENS = 512
N_EXPERT = 4
N_TENSOR = 2


def hot_choice(key):
    hot_count = 1 + jax.random.randint(jax.random.fold_in(key, 11), (), 0, 2)
    hot_order = jax.random.permutation(jax.random.fold_in(key, 12), EXPERTS).astype(jnp.int32)
    order_rank = jnp.zeros((EXPERTS,), jnp.int32).at[hot_order].set(jnp.arange(EXPERTS, dtype=jnp.int32))
    return ((order_rank < hot_count).astype(jnp.int32), hot_order, hot_count)


def draw_popular_specialist_flags(key, part):
    flags, hot_order, hot_count = hot_choice(key)
    return flags


def draw_group_quotas(key, part):
    flags, hot_order, hot_count = hot_choice(key)
    key = jax.random.fold_in(key, 5)
    lowest = max(GROUP_QUOTA // 4, 2)
    highest = GROUP_QUOTA // 2
    drawn_caps = jax.random.randint(key, (EXPERTS,), lowest, highest + 1).astype(jnp.int32)
    drawn_caps = drawn_caps.at[hot_order[2]].set(lowest)
    drawn_caps = drawn_caps.at[hot_order[3]].set(highest)
    return drawn_caps.astype(jnp.int32)


def draw_routed_specialist_pairs(key, part):
    flags, hot_order, hot_count = hot_choice(key)
    key = jax.random.fold_in(key, 3)
    blocks = TOKENS // TOK
    block_keys = jax.random.split(jax.random.fold_in(key, 1), blocks)
    places = jax.vmap(lambda sub_key: jax.random.permutation(sub_key, TOK))(block_keys).astype(jnp.int32)
    hot_pick = hot_order[jnp.minimum(places // GROUP_QUOTA, EXPERTS - 1)]
    free_pick = jax.random.randint(jax.random.fold_in(key, 2), (blocks, TOK), 0, EXPERTS)
    first_pick = jnp.where(places < GROUP_QUOTA * hot_count, hot_pick, free_pick)
    shift_by = jax.random.randint(jax.random.fold_in(key, 4), (blocks, TOK), 1, EXPERTS)
    second = (first_pick + shift_by) % EXPERTS
    return jnp.stack([first_pick, second], axis=-1).reshape(TOKENS, 2).astype(jnp.int32)


def block_levels(rng, extent, cuts, low, high):
    gain = 1.0
    for position, blocks in cuts:
        draws = jax.random.uniform(jax.random.fold_in(jax.random.fold_in(rng, 6), position), (blocks,), jnp.float32, low / len(cuts), high / len(cuts))
        gain = gain * jnp.repeat(jnp.exp(draws), extent[position] // blocks).reshape((-1,) + (1,) * (len(extent) - 1 - position))
    return gain


def scatter_about(stream_key, extent, deviation, bound, cuts=(), kind=jnp.bfloat16):
    drawn = jax.random.normal(stream_key, extent, jnp.float32) * deviation
    if len(cuts) > 0:
        drawn = block_levels(stream_key, extent, cuts, -0.22, 0.18) * drawn
    return jnp.clip(drawn, min=-bound, max=bound).astype(kind)


def setup_inputs(seed: int = 0, part: int = 0) -> dict:
    key_list = jax.random.split(jax.random.key(seed), 9)
    own_keys = jax.random.split(jax.random.fold_in(key_list[8], part), 9)
    incoming_activation_vectors = scatter_about(own_keys[0], (TOKENS, D), 1.0, 6.0, ((0, 8), (1, 2)))
    routed_specialist_pairs = draw_routed_specialist_pairs(jax.random.fold_in(jax.random.fold_in(key_list[8], part), 71), part)
    routing_shares = jnp.clip(0.2 + 0.8 * jax.random.uniform(own_keys[2], (TOKENS, 2), jnp.float32) ** block_levels(own_keys[2], (TOKENS, 2), ((0, 8),), -0.2, 0.2), 0.2, 1.0)
    popular_specialist_flags = draw_popular_specialist_flags(jax.random.fold_in(jax.random.fold_in(key_list[8], part), 71), part)
    group_quotas = draw_group_quotas(jax.random.fold_in(jax.random.fold_in(key_list[8], part), 71), part)
    gating_weight_stack = scatter_about(key_list[5], (D, EXPERTS * F), D ** -0.5, 0.109375, ((0, 2), (1, 8)))
    widen_weight_stack = scatter_about(key_list[6], (D, EXPERTS * F), D ** -0.5, 0.109375, ((0, 2), (1, 8)))
    contract_weight_stack = scatter_about(key_list[7], (EXPERTS * F, D), F ** -0.5, 0.0625, ((0, 8), (1, 2)))
    return dict(incoming_activation_vectors=incoming_activation_vectors, routed_specialist_pairs=routed_specialist_pairs, routing_shares=routing_shares, popular_specialist_flags=popular_specialist_flags, group_quotas=group_quotas, gating_weight_stack=gating_weight_stack, widen_weight_stack=widen_weight_stack, contract_weight_stack=contract_weight_stack)


def expert_output(inputs):
    block_rows, gate_part, up_part, down_part = inputs
    gate_sum = jnp.dot(block_rows, gate_part, preferred_element_type=jnp.float32)
    up_sum = jnp.dot(block_rows, up_part, preferred_element_type=jnp.float32)
    hidden = (jax.nn.silu(gate_sum) * up_sum).astype(jnp.bfloat16)
    unit_blocks = N_EXPERT * N_TENSOR // EXPERTS
    unit_width = F // unit_blocks
    hidden_blocks = hidden.reshape(hidden.shape[0], unit_blocks, unit_width).transpose(1, 0, 2)
    down_blocks = down_part.reshape(unit_blocks, unit_width, D)

    def add_block(total, operands):
        term = jnp.dot(operands[0], operands[1], preferred_element_type=jnp.float32).astype(jnp.bfloat16)
        term = lax.optimization_barrier(term)
        return total + term.astype(jnp.float32), None

    start_total = jnp.zeros((hidden.shape[0], D), jnp.float32)
    total, unused = lax.scan(add_block, start_total, (hidden_blocks, down_blocks))
    return total


def reference(incoming_activation_vectors, routed_specialist_pairs, routing_shares, popular_specialist_flags, group_quotas, gating_weight_stack, widen_weight_stack, contract_weight_stack):
    blocks = TOKENS // TOK
    pair_ids = routed_specialist_pairs.reshape(blocks, TOK * 2)
    onehot = (pair_ids[:, :, None] == jnp.arange(EXPERTS, dtype=jnp.int32)[None, None, :]).astype(jnp.int32)
    earlier = jnp.cumsum(onehot, axis=1) - onehot
    slot_rank = jnp.sum(earlier * onehot, axis=2)
    quota_bound = jnp.where(popular_specialist_flags == 1, GROUP_QUOTA, group_quotas).astype(jnp.int32)
    kept_pair = slot_rank < quota_bound[pair_ids]
    block_index = jnp.arange(blocks, dtype=jnp.int32)[:, None]
    token_index = block_index * TOK + jnp.arange(TOK * 2, dtype=jnp.int32)[None, :] // 2
    dump = EXPERTS * blocks * GROUP_QUOTA
    target = jnp.where(kept_pair, pair_ids * (blocks * GROUP_QUOTA) + block_index * GROUP_QUOTA + slot_rank, dump).astype(jnp.int32)
    row_source = jnp.zeros((dump + 1,), jnp.int32).at[target.reshape(-1)].set(token_index.reshape(-1) + 1)[:dump]
    owner_rows = jnp.where((row_source > 0)[:, None], incoming_activation_vectors[jnp.maximum(row_source - 1, 0)], 0).astype(jnp.bfloat16)
    gate_parts = gating_weight_stack.reshape(D, EXPERTS, F).transpose(1, 0, 2)
    up_parts = widen_weight_stack.reshape(D, EXPERTS, F).transpose(1, 0, 2)
    down_parts = contract_weight_stack.reshape(EXPERTS, F, D)
    outs = lax.map(expert_output, (owner_rows.reshape(EXPERTS, blocks * GROUP_QUOTA, D), gate_parts, up_parts, down_parts))
    flat_out = outs.reshape(-1, D)
    pick_index = jnp.where(kept_pair, target, 0).reshape(TOKENS, 2)
    weights_kept = jnp.where(kept_pair.reshape(TOKENS, 2), routing_shares, 0.0).astype(jnp.float32)
    mixed = weights_kept[:, 0:1] * flat_out[pick_index[:, 0]] + weights_kept[:, 1:2] * flat_out[pick_index[:, 1]]
    return mixed.astype(jnp.bfloat16)
```

```python
import jax
import jax.numpy as jnp
from jax import lax
from jax.sharding import PartitionSpec as P

GROUP_QUOTA = 32
EXPERTS = 4


def gathered(
    incoming_activation_vectors,
    routed_specialist_pairs,
    routing_shares,
    popular_specialist_flags,
    group_quotas,
    gating_weight_stack,
    widen_weight_stack,
    contract_weight_stack,
):
    experts = popular_specialist_flags.shape[0]
    tok_rows = incoming_activation_vectors.shape[0]
    half_width = incoming_activation_vectors.shape[1]
    expert_count = lax.axis_size("expert")
    tensor_count = lax.axis_size("tensor")
    owners = expert_count // experts
    pair_ids = routed_specialist_pairs.reshape(-1)
    onehot = (pair_ids[:, None] == jnp.arange(experts, dtype=jnp.int32)[None, :]).astype(jnp.int32)
    slot_rank = jnp.sum((jnp.cumsum(onehot, axis=0) - onehot) * onehot, axis=1)
    quota_bound = jnp.where(popular_specialist_flags == 1, GROUP_QUOTA, group_quotas)
    kept_pair = slot_rank < jnp.sum(onehot * quota_bound[None, :], axis=1)
    target = jnp.where(kept_pair, pair_ids * GROUP_QUOTA + slot_rank, -1)
    select = (
        jnp.arange(experts * GROUP_QUOTA, dtype=jnp.int32)[:, None] == target[None, :]
    ).astype(jnp.bfloat16)
    select = select.reshape(experts * GROUP_QUOTA, tok_rows, 2).sum(axis=2)
    packed = jnp.dot(
        select, incoming_activation_vectors, preferred_element_type=jnp.float32
    ).astype(jnp.bfloat16)
    packed = packed.reshape(experts, GROUP_QUOTA, half_width)
    outgoing = jnp.repeat(packed, owners * tensor_count, axis=0)
    arrived = lax.all_to_all(
        outgoing, ("expert", "tensor"), split_axis=0, concat_axis=2, tiled=True
    )
    owner_rows = arrived.reshape(GROUP_QUOTA * expert_count, half_width * tensor_count)
    gate_part = jnp.dot(
        owner_rows,
        lax.all_gather(gating_weight_stack, "dp", axis=0, tiled=True),
        preferred_element_type=jnp.float32,
    )
    up_part = jnp.dot(
        owner_rows,
        lax.all_gather(widen_weight_stack, "dp", axis=0, tiled=True),
        preferred_element_type=jnp.float32,
    )
    hidden = (jax.nn.silu(gate_part) * up_part).astype(jnp.bfloat16)
    partial_value = jnp.dot(
        hidden,
        lax.all_gather(contract_weight_stack, "dp", axis=1, tiled=True),
        preferred_element_type=jnp.float32,
    )
    partial_value = partial_value.astype(jnp.bfloat16).reshape(
        1, GROUP_QUOTA, expert_count * tensor_count * half_width
    )
    returned = lax.all_to_all(
        partial_value, ("expert", "tensor"), split_axis=2, concat_axis=0, tiled=True
    )
    summed = (
        returned.astype(jnp.float32)
        .reshape(experts, owners * tensor_count, GROUP_QUOTA, half_width)
        .sum(axis=1)
    )
    summed = summed.reshape(experts * GROUP_QUOTA, half_width)
    pick_index = jnp.maximum(target, 0)
    weights_kept = jnp.where(kept_pair, routing_shares.reshape(-1), 0.0)
    picked = jnp.take(summed, pick_index, axis=0) * weights_kept[:, None]
    mixed = picked.reshape(tok_rows, 2, half_width).sum(axis=1)
    return mixed.astype(jnp.bfloat16)


def route(routed_specialist_pairs, popular_specialist_flags, group_quotas):
    experts = popular_specialist_flags.shape[0]
    pair_ids = routed_specialist_pairs.reshape(-1)
    onehot = (pair_ids[:, None] == jnp.arange(experts, dtype=jnp.int32)[None, :]).astype(jnp.int32)
    slot_rank = jnp.sum((jnp.cumsum(onehot, axis=0) - onehot) * onehot, axis=1)
    quota_bound = jnp.where(popular_specialist_flags == 1, GROUP_QUOTA, group_quotas)
    kept_pair = slot_rank < jnp.sum(onehot * quota_bound[None, :], axis=1)
    return kept_pair, jnp.where(kept_pair, pair_ids * GROUP_QUOTA + slot_rank, -1)


CHUNKS = 4
SWAP = [(d * 2 + t, t * 2 + d) for d in range(2) for t in range(2)]


def partial_sums(
    incoming_activation_vectors,
    routed_specialist_pairs,
    routing_shares,
    popular_specialist_flags,
    group_quotas,
    gating_weight_stack,
    widen_weight_stack,
    contract_weight_stack,
):
    experts = popular_specialist_flags.shape[0]
    tok_rows, half_width = incoming_activation_vectors.shape
    units = gating_weight_stack.shape[1]
    kept_pair, target = route(routed_specialist_pairs, popular_specialist_flags, group_quotas)
    slots = experts * GROUP_QUOTA
    hits = jnp.arange(slots, dtype=jnp.int32)[:, None] == target[None, :]
    hits = hits.reshape(slots, tok_rows, 2)
    select = hits.astype(jnp.bfloat16).sum(axis=2)
    packed = jnp.dot(
        select, incoming_activation_vectors, preferred_element_type=jnp.float32
    ).astype(jnp.bfloat16)
    packed = lax.all_to_all(
        packed.reshape(experts, GROUP_QUOTA, half_width), "expert", 0, 0, tiled=True
    )
    packed = lax.ppermute(packed.reshape(slots, half_width), ("dp", "tensor"), SWAP)
    rows = lax.all_gather(packed, "tensor", axis=0, tiled=True)
    me = lax.axis_index("dp")
    swapped = [(0, 1), (1, 0)]
    own = lax.dynamic_slice_in_dim(rows, me * slots, slots, 0)
    other = lax.dynamic_slice_in_dim(rows, (1 - me) * slots, slots, 0)
    rows = jnp.concatenate([own, other], axis=0)
    width = units // CHUNKS
    out = jnp.zeros((2 * slots, half_width), jnp.float32)
    pieces = []
    for chunk in range(CHUNKS):
        cols = slice(chunk * width, (chunk + 1) * width)
        gate = jnp.dot(rows, gating_weight_stack[:, cols], preferred_element_type=jnp.float32)
        up = jnp.dot(rows, widen_weight_stack[:, cols], preferred_element_type=jnp.float32)
        away = jnp.concatenate([gate[slots:], up[slots:]], axis=1).astype(jnp.bfloat16)
        came = lax.ppermute(away, "dp", swapped).astype(jnp.float32)
        gate = gate[:slots] + came[:, :width]
        up = up[:slots] + came[:, width:]
        hidden = (jax.nn.silu(gate) * up).astype(jnp.bfloat16)
        pieces.append((hidden, lax.ppermute(hidden, "dp", swapped)))
    mine = jnp.concatenate([a for a, b in pieces], axis=1)
    theirs = jnp.concatenate([b for a, b in pieces], axis=1)
    out_mine = jnp.dot(mine, contract_weight_stack, preferred_element_type=jnp.float32).astype(jnp.bfloat16)
    out_theirs = jnp.dot(theirs, contract_weight_stack, preferred_element_type=jnp.float32).astype(jnp.bfloat16)
    core = lax.axis_index("tensor")
    keep = jnp.where(core == me, out_mine, out_theirs)
    send = jnp.where(core == me, out_theirs, out_mine)
    got = lax.ppermute(send, "tensor", swapped)
    total = (keep.astype(jnp.float32) + got.astype(jnp.float32)).astype(jnp.bfloat16)
    total = lax.ppermute(total, ("dp", "tensor"), SWAP)
    summed = lax.all_to_all(
        total.reshape(experts, GROUP_QUOTA, half_width), "expert", 0, 0, tiled=True
    ).reshape(slots, half_width)
    weights_kept = jnp.where(kept_pair, routing_shares.reshape(-1), 0.0)
    pick = jnp.where(hits, weights_kept.reshape(1, tok_rows, 2), 0.0).sum(axis=2)
    return jnp.dot(
        pick.T, summed.astype(jnp.float32), precision=lax.Precision.HIGHEST
    ).astype(jnp.bfloat16)


def solution(mesh):
    shape = mesh.shape
    square = shape["dp"] == 2 and shape["tensor"] == 2 and shape["expert"] == EXPERTS
    local = partial_sums if square else gathered
    placed = (
        P(("group", "expert", "dp"), "tensor"),
        P(("group", "expert", "dp"), None),
        P(("group", "expert", "dp"), None),
        P("group"),
        P("group"),
        P("dp", ("expert", "tensor")),
        P("dp", ("expert", "tensor")),
        P(("expert", "tensor"), "dp"),
    )
    return jax.shard_map(
        local,
        mesh=mesh,
        in_specs=placed,
        out_specs=P(("group", "expert", "dp"), "tensor"),
        check_vma=False,
    )
```

```python
import jax
import jax.numpy as jnp
from jax import lax
from jax.experimental import pallas as pl
from jax.experimental.pallas import tpu as pltpu
from jax.sharding import PartitionSpec as P

GROUP_QUOTA = 32
EXPERTS = 4


def gathered(
    incoming_activation_vectors,
    routed_specialist_pairs,
    routing_shares,
    popular_specialist_flags,
    group_quotas,
    gating_weight_stack,
    widen_weight_stack,
    contract_weight_stack,
):
    experts = popular_specialist_flags.shape[0]
    tok_rows = incoming_activation_vectors.shape[0]
    half_width = incoming_activation_vectors.shape[1]
    expert_count = lax.axis_size("expert")
    tensor_count = lax.axis_size("tensor")
    owners = expert_count // experts
    pair_ids = routed_specialist_pairs.reshape(-1)
    onehot = (pair_ids[:, None] == jnp.arange(experts, dtype=jnp.int32)[None, :]).astype(jnp.int32)
    slot_rank = jnp.sum((jnp.cumsum(onehot, axis=0) - onehot) * onehot, axis=1)
    quota_bound = jnp.where(popular_specialist_flags == 1, GROUP_QUOTA, group_quotas)
    kept_pair = slot_rank < jnp.sum(onehot * quota_bound[None, :], axis=1)
    target = jnp.where(kept_pair, pair_ids * GROUP_QUOTA + slot_rank, -1)
    select = (
        jnp.arange(experts * GROUP_QUOTA, dtype=jnp.int32)[:, None] == target[None, :]
    ).astype(jnp.bfloat16)
    select = select.reshape(experts * GROUP_QUOTA, tok_rows, 2).sum(axis=2)
    packed = jnp.dot(
        select, incoming_activation_vectors, preferred_element_type=jnp.float32
    ).astype(jnp.bfloat16)
    packed = packed.reshape(experts, GROUP_QUOTA, half_width)
    outgoing = jnp.repeat(packed, owners * tensor_count, axis=0)
    arrived = lax.all_to_all(
        outgoing, ("expert", "tensor"), split_axis=0, concat_axis=2, tiled=True
    )
    owner_rows = arrived.reshape(GROUP_QUOTA * expert_count, half_width * tensor_count)
    gate_part = jnp.dot(
        owner_rows,
        lax.all_gather(gating_weight_stack, "dp", axis=0, tiled=True),
        preferred_element_type=jnp.float32,
    )
    up_part = jnp.dot(
        owner_rows,
        lax.all_gather(widen_weight_stack, "dp", axis=0, tiled=True),
        preferred_element_type=jnp.float32,
    )
    hidden = (jax.nn.silu(gate_part) * up_part).astype(jnp.bfloat16)
    partial_value = jnp.dot(
        hidden,
        lax.all_gather(contract_weight_stack, "dp", axis=1, tiled=True),
        preferred_element_type=jnp.float32,
    )
    partial_value = partial_value.astype(jnp.bfloat16).reshape(
        1, GROUP_QUOTA, expert_count * tensor_count * half_width
    )
    returned = lax.all_to_all(
        partial_value, ("expert", "tensor"), split_axis=2, concat_axis=0, tiled=True
    )
    summed = (
        returned.astype(jnp.float32)
        .reshape(experts, owners * tensor_count, GROUP_QUOTA, half_width)
        .sum(axis=1)
    )
    summed = summed.reshape(experts * GROUP_QUOTA, half_width)
    pick_index = jnp.maximum(target, 0)
    weights_kept = jnp.where(kept_pair, routing_shares.reshape(-1), 0.0)
    picked = jnp.take(summed, pick_index, axis=0) * weights_kept[:, None]
    mixed = picked.reshape(tok_rows, 2, half_width).sum(axis=1)
    return mixed.astype(jnp.bfloat16)


def route(routed_specialist_pairs, popular_specialist_flags, group_quotas):
    experts = popular_specialist_flags.shape[0]
    pair_ids = routed_specialist_pairs.reshape(-1)
    onehot = (pair_ids[:, None] == jnp.arange(experts, dtype=jnp.int32)[None, :]).astype(jnp.int32)
    slot_rank = jnp.sum((jnp.cumsum(onehot, axis=0) - onehot) * onehot, axis=1)
    quota_bound = jnp.where(popular_specialist_flags == 1, GROUP_QUOTA, group_quotas)
    kept_pair = slot_rank < jnp.sum(onehot * quota_bound[None, :], axis=1)
    return kept_pair, jnp.where(kept_pair, pair_ids * GROUP_QUOTA + slot_rank, -1)


HOPS = 4
PARTS = 4
STEPS = HOPS * PARTS
LAG_SUM = 3
LAG_DOWN = 3


def flip(e, k):
    low = lax.rem(lax.rem(e, 2) + lax.rem(k, 2), 2)
    high = lax.rem(lax.div(e, 2) + lax.div(k, 2), 2)
    return low + 2 * high


def layer_kernel(
    packed,
    gate_hbm,
    up_hbm,
    down_hbm,
    out,
    gate_w,
    up_w,
    down_w,
    rows,
    keep,
    part_out,
    part_in,
    hid,
    acc,
    core_in,
    back,
    w_sem,
    disp_send,
    disp_recv,
    fwd_send,
    fwd_recv,
    self_sem,
    part_send,
    part_recv,
    hid_send,
    hid_recv,
    core_send,
    core_recv,
    back_send,
    back_recv,
):
    e = lax.axis_index("expert")
    d = lax.axis_index("dp")
    t = lax.axis_index("tensor")
    quota = packed.shape[1]
    width = gate_w.shape[2]
    mesh_ids = pl.DeviceIdType.MESH
    home = d == t
    direct = lax.rem(d + t, 2)

    def weight_copy(which, j):
        hbm, vmem = ((gate_hbm, gate_w), (up_hbm, up_w), (down_hbm, down_w))[which]
        start = pl.multiple_of(j * width, width)
        block = hbm.at[pl.ds(start, width), :] if which == 2 else hbm.at[:, pl.ds(start, width)]
        return pltpu.make_async_copy(block, vmem.at[j], w_sem.at[which, j])

    def far(k):
        return {"expert": flip(e, k), "dp": t, "tensor": d}

    sibling = {"expert": e, "dp": d, "tensor": 1 - t}
    across = {"expert": e, "dp": 1 - d, "tensor": t}

    def remote(src, dst, send, recv, target):
        return pltpu.make_async_remote_copy(
            src_ref=src,
            dst_ref=dst,
            send_sem=send,
            recv_sem=recv,
            device_id=target,
            device_id_type=mesh_ids,
        )

    def dispatch(k):
        return remote(
            packed.at[k], rows.at[k, direct], disp_send.at[k], disp_recv.at[k], far(k)
        )

    def dispatch_self():
        return pltpu.make_async_copy(packed.at[0], rows.at[0, direct], self_sem)

    def forward(k):
        return remote(
            rows.at[k, direct], rows.at[k, direct], fwd_send.at[k], fwd_recv.at[k], sibling
        )

    def part_copy(s):
        return remote(part_out.at[s], part_in.at[s], part_send.at[s], part_recv.at[s], across)

    def hid_copy(s):
        return remote(hid.at[s, 0], hid.at[s, 1], hid_send.at[s], hid_recv.at[s], across)

    def core_copy(k):
        return remote(acc.at[k, 1 - direct], core_in.at[k], core_send.at[k], core_recv.at[k], sibling)

    def back_copy(k):
        return remote(back.at[k], out.at[k], back_send.at[k], back_recv.at[k], far(k))

    for j in range(PARTS):
        weight_copy(0, j).start()
        weight_copy(1, j).start()
    for j in range(PARTS):
        weight_copy(2, j).start()

    barrier = pltpu.get_barrier_semaphore()
    for target in (sibling, across, far(1), far(2), far(3)):
        pl.semaphore_signal(barrier, inc=1, device_id=target, device_id_type=mesh_ids)

    @pl.when(home)
    def _():
        pl.semaphore_wait(barrier, 5)
        dispatch_self().start()

    @pl.when(jnp.logical_not(home))
    def _():
        pl.semaphore_signal(barrier, inc=1, device_id=far(0), device_id_type=mesh_ids)
        pl.semaphore_wait(barrier, 6)
        dispatch(0).start()

    for k in range(1, HOPS):
        dispatch(k).start()

    @pl.when(home)
    def _():
        dispatch_self().wait()

    @pl.when(jnp.logical_not(home))
    def _():
        dispatch(0).wait_recv()

    forward(0).start()
    forward(0).wait_recv()

    def body(s, carry):
        k = lax.div(s, PARTS)
        j = lax.rem(s, PARTS)

        @pl.when(s < STEPS)
        def _():
            @pl.when(jnp.logical_and(j == 0, k > 0))
            def _():
                forward(k).wait_recv()

            @pl.when(k == 0)
            def _():
                weight_copy(0, j).wait()
                weight_copy(1, j).wait()

            block = rows[k].reshape(2 * quota, rows.shape[3])
            gate = jnp.dot(block, gate_w[j], preferred_element_type=jnp.float32)
            keep[s, 0] = gate[:quota]
            part_out[s, 0] = gate[quota:].astype(jnp.bfloat16)
            up = jnp.dot(block, up_w[j], preferred_element_type=jnp.float32)
            keep[s, 1] = up[:quota]
            part_out[s, 1] = up[quota:].astype(jnp.bfloat16)
            part_copy(s).start()

            @pl.when(jnp.logical_and(j == PARTS // 2, k < HOPS - 1))
            def _():
                dispatch(k + 1).wait_recv()
                forward(k + 1).start()

        h = s - LAG_SUM

        @pl.when(jnp.logical_and(h >= 0, h < STEPS))
        def _():
            part_copy(h).wait_recv()
            gate = keep[h, 0] + part_in[h, 0].astype(jnp.float32)
            up = keep[h, 1] + part_in[h, 1].astype(jnp.float32)
            hid[h, 0] = (gate / (1.0 + jnp.exp(-gate)) * up).astype(jnp.bfloat16)
            hid_copy(h).start()

        q = s - LAG_SUM - LAG_DOWN

        @pl.when(q >= 0)
        def _():
            kq = lax.div(q, PARTS)
            jq = lax.rem(q, PARTS)
            hid_copy(q).wait_recv()

            @pl.when(kq == 0)
            def _():
                weight_copy(2, jq).wait()

            term = jnp.dot(
                hid[q].reshape(2 * quota, width), down_w[jq], preferred_element_type=jnp.float32
            ).reshape(2, quota, acc.shape[3])

            @pl.when(jq == 0)
            def _():
                acc[kq] = term

            @pl.when(jq > 0)
            def _():
                acc[kq] = acc[kq] + term

            @pl.when(jq == PARTS - 1)
            def _():
                core_copy(kq).start()
                core_copy(kq).wait_recv()
                total = (acc[kq, direct] + core_in[kq]).astype(jnp.bfloat16)
                stays = jnp.logical_and(home, kq == 0)

                @pl.when(stays)
                def _():
                    out[0] = total

                @pl.when(jnp.logical_not(stays))
                def _():
                    back[kq] = total
                    back_copy(kq).start()

        return carry

    lax.fori_loop(0, STEPS + LAG_SUM + LAG_DOWN, body, 0)

    def drain(s, carry):
        part_copy(s).wait_send()
        hid_copy(s).wait_send()
        return carry

    lax.fori_loop(0, STEPS, drain, 0)
    for k in range(HOPS):
        forward(k).wait_send()
        core_copy(k).wait_send()
        if k > 0:
            dispatch(k).wait_send()
            back_copy(k).wait()

    @pl.when(jnp.logical_not(home))
    def _():
        dispatch(0).wait_send()
        back_copy(0).wait()


def fused(
    incoming_activation_vectors,
    routed_specialist_pairs,
    routing_shares,
    popular_specialist_flags,
    group_quotas,
    gating_weight_stack,
    widen_weight_stack,
    contract_weight_stack,
):
    experts = popular_specialist_flags.shape[0]
    tok_rows, half_width = incoming_activation_vectors.shape
    units = gating_weight_stack.shape[1]
    width = units // PARTS
    kept_pair, target = route(routed_specialist_pairs, popular_specialist_flags, group_quotas)
    slots = experts * GROUP_QUOTA
    place = jnp.arange(slots, dtype=jnp.int32)
    place = (place // GROUP_QUOTA ^ lax.axis_index("expert")) * GROUP_QUOTA + place % GROUP_QUOTA
    hits = (place[:, None] == target[None, :]).reshape(slots, tok_rows, 2)
    select = hits.astype(jnp.bfloat16).sum(axis=2)
    packed = jnp.dot(
        select, incoming_activation_vectors, preferred_element_type=jnp.float32
    ).astype(jnp.bfloat16)
    bf16, f32 = jnp.bfloat16, jnp.float32
    dma = pltpu.SemaphoreType.DMA
    quota = GROUP_QUOTA
    summed = pl.pallas_call(
        layer_kernel,
        out_shape=jax.ShapeDtypeStruct((HOPS, quota, half_width), bf16),
        in_specs=[pl.BlockSpec(memory_space=pltpu.VMEM)] + [pl.BlockSpec(memory_space=pl.ANY)] * 3,
        out_specs=pl.BlockSpec(memory_space=pltpu.VMEM),
        scratch_shapes=[
            pltpu.VMEM((PARTS, half_width, width), bf16),
            pltpu.VMEM((PARTS, half_width, width), bf16),
            pltpu.VMEM((PARTS, width, half_width), bf16),
            pltpu.VMEM((HOPS, 2, quota, half_width), bf16),
            pltpu.VMEM((STEPS, 2, quota, width), f32),
            pltpu.VMEM((STEPS, 2, quota, width), bf16),
            pltpu.VMEM((STEPS, 2, quota, width), bf16),
            pltpu.VMEM((STEPS, 2, quota, width), bf16),
            pltpu.VMEM((HOPS, 2, quota, half_width), f32),
            pltpu.VMEM((HOPS, quota, half_width), f32),
            pltpu.VMEM((HOPS, quota, half_width), bf16),
            dma((3, PARTS)),
            dma((HOPS,)),
            dma((HOPS,)),
            dma((HOPS,)),
            dma((HOPS,)),
            dma,
            dma((STEPS,)),
            dma((STEPS,)),
            dma((STEPS,)),
            dma((STEPS,)),
            dma((HOPS,)),
            dma((HOPS,)),
            dma((HOPS,)),
            dma((HOPS,)),
        ],
        compiler_params=pltpu.CompilerParams(
            collective_id=0, has_side_effects=True, vmem_limit_bytes=60 * 1024 * 1024
        ),
        name="expert_layer",
    )(
        packed.reshape(HOPS, quota, half_width),
        gating_weight_stack,
        widen_weight_stack,
        contract_weight_stack,
    )
    weights_kept = jnp.where(kept_pair, routing_shares.reshape(-1), 0.0)
    pick = jnp.where(hits, weights_kept.reshape(1, tok_rows, 2), 0.0).sum(axis=2)
    return jnp.dot(
        pick.T,
        summed.reshape(slots, half_width).astype(jnp.float32),
        precision=lax.Precision.HIGHEST,
    ).astype(jnp.bfloat16)


def solution(mesh):
    shape = mesh.shape
    square = shape["dp"] == 2 and shape["tensor"] == 2 and shape["expert"] == EXPERTS
    local = fused if square else gathered
    placed = (
        P(("group", "expert", "dp"), "tensor"),
        P(("group", "expert", "dp"), None),
        P(("group", "expert", "dp"), None),
        P("group"),
        P("group"),
        P("dp", ("expert", "tensor")),
        P("dp", ("expert", "tensor")),
        P(("expert", "tensor"), "dp"),
    )
    return jax.shard_map(
        local,
        mesh=mesh,
        in_specs=placed,
        out_specs=P(("group", "expert", "dp"), "tensor"),
        check_vma=False,
    )
```

```python
import jax
import jax.numpy as jnp
from jax import lax
from jax.experimental import pallas as pl
from jax.experimental.pallas import tpu as pltpu
from jax.sharding import PartitionSpec as P

GROUP_QUOTA = 32
EXPERTS = 4


def gathered(
    incoming_activation_vectors,
    routed_specialist_pairs,
    routing_shares,
    popular_specialist_flags,
    group_quotas,
    gating_weight_stack,
    widen_weight_stack,
    contract_weight_stack,
):
    experts = popular_specialist_flags.shape[0]
    tok_rows = incoming_activation_vectors.shape[0]
    half_width = incoming_activation_vectors.shape[1]
    expert_count = lax.axis_size("expert")
    tensor_count = lax.axis_size("tensor")
    owners = expert_count // experts
    pair_ids = routed_specialist_pairs.reshape(-1)
    onehot = (pair_ids[:, None] == jnp.arange(experts, dtype=jnp.int32)[None, :]).astype(jnp.int32)
    slot_rank = jnp.sum((jnp.cumsum(onehot, axis=0) - onehot) * onehot, axis=1)
    quota_bound = jnp.where(popular_specialist_flags == 1, GROUP_QUOTA, group_quotas)
    kept_pair = slot_rank < jnp.sum(onehot * quota_bound[None, :], axis=1)
    target = jnp.where(kept_pair, pair_ids * GROUP_QUOTA + slot_rank, -1)
    select = (
        jnp.arange(experts * GROUP_QUOTA, dtype=jnp.int32)[:, None] == target[None, :]
    ).astype(jnp.bfloat16)
    select = select.reshape(experts * GROUP_QUOTA, tok_rows, 2).sum(axis=2)
    packed = jnp.dot(
        select, incoming_activation_vectors, preferred_element_type=jnp.float32
    ).astype(jnp.bfloat16)
    packed = packed.reshape(experts, GROUP_QUOTA, half_width)
    outgoing = jnp.repeat(packed, owners * tensor_count, axis=0)
    arrived = lax.all_to_all(
        outgoing, ("expert", "tensor"), split_axis=0, concat_axis=2, tiled=True
    )
    owner_rows = arrived.reshape(GROUP_QUOTA * expert_count, half_width * tensor_count)
    gate_part = jnp.dot(
        owner_rows,
        lax.all_gather(gating_weight_stack, "dp", axis=0, tiled=True),
        preferred_element_type=jnp.float32,
    )
    up_part = jnp.dot(
        owner_rows,
        lax.all_gather(widen_weight_stack, "dp", axis=0, tiled=True),
        preferred_element_type=jnp.float32,
    )
    hidden = (jax.nn.silu(gate_part) * up_part).astype(jnp.bfloat16)
    partial_value = jnp.dot(
        hidden,
        lax.all_gather(contract_weight_stack, "dp", axis=1, tiled=True),
        preferred_element_type=jnp.float32,
    )
    partial_value = partial_value.astype(jnp.bfloat16).reshape(
        1, GROUP_QUOTA, expert_count * tensor_count * half_width
    )
    returned = lax.all_to_all(
        partial_value, ("expert", "tensor"), split_axis=2, concat_axis=0, tiled=True
    )
    summed = (
        returned.astype(jnp.float32)
        .reshape(experts, owners * tensor_count, GROUP_QUOTA, half_width)
        .sum(axis=1)
    )
    summed = summed.reshape(experts * GROUP_QUOTA, half_width)
    pick_index = jnp.maximum(target, 0)
    weights_kept = jnp.where(kept_pair, routing_shares.reshape(-1), 0.0)
    picked = jnp.take(summed, pick_index, axis=0) * weights_kept[:, None]
    mixed = picked.reshape(tok_rows, 2, half_width).sum(axis=1)
    return mixed.astype(jnp.bfloat16)


HOPS = 4
PARTS = 4
STEPS = HOPS * PARTS
LAG_SUM = 3
LAG_DOWN = 3
AHEAD = 2


def flip(e, k):
    low = lax.rem(lax.rem(e, 2) + lax.rem(k, 2), 2)
    high = lax.rem(lax.div(e, 2) + lax.div(k, 2), 2)
    return low + 2 * high


def layer_kernel(
    flags,
    quotas,
    tokens,
    pairs,
    shares,
    gate_hbm,
    up_hbm,
    down_hbm,
    out,
    gate_w,
    up_w,
    down_w,
    packed,
    picks,
    returned,
    rows,
    keep,
    part_out,
    part_in,
    hid,
    acc,
    core_in,
    back,
    w_sem,
    disp_send,
    disp_recv,
    fwd_send,
    fwd_recv,
    part_send,
    part_recv,
    hid_send,
    hid_recv,
    core_send,
    core_recv,
    back_send,
    back_recv,
):
    e = lax.axis_index("expert")
    d = lax.axis_index("dp")
    t = lax.axis_index("tensor")
    quota = packed.shape[1]
    width = gate_w.shape[2]
    mesh_ids = pl.DeviceIdType.MESH
    home = d == t
    direct = lax.rem(d + t, 2)

    def weight_copy(which, j):
        hbm, vmem = ((gate_hbm, gate_w), (up_hbm, up_w), (down_hbm, down_w))[which]
        start = pl.multiple_of(j * width, width)
        block = hbm.at[pl.ds(start, width), :] if which == 2 else hbm.at[:, pl.ds(start, width)]
        return pltpu.make_async_copy(block, vmem.at[j], w_sem.at[which, j])

    def far(k):
        return {"expert": flip(e, k), "dp": t, "tensor": d}

    sibling = {"expert": e, "dp": d, "tensor": 1 - t}
    across = {"expert": e, "dp": 1 - d, "tensor": t}

    def remote(src, dst, send, recv, target):
        return pltpu.make_async_remote_copy(
            src_ref=src,
            dst_ref=dst,
            send_sem=send,
            recv_sem=recv,
            device_id=target,
            device_id_type=mesh_ids,
        )

    def dispatch(k):
        return remote(
            packed.at[k], rows.at[k, direct], disp_send.at[k], disp_recv.at[k], far(k)
        )

    def forward(k):
        return remote(
            rows.at[k, direct], rows.at[k, direct], fwd_send.at[k], fwd_recv.at[k], sibling
        )

    def part_copy(s):
        return remote(part_out.at[s], part_in.at[s], part_send.at[s], part_recv.at[s], across)

    def hid_copy(s):
        return remote(hid.at[s, 0], hid.at[s, 1], hid_send.at[s], hid_recv.at[s], across)

    def core_copy(k):
        return remote(acc.at[k, 1 - direct], core_in.at[k], core_send.at[k], core_recv.at[k], sibling)

    def back_copy(k):
        return remote(back.at[k], returned.at[k], back_send.at[k], back_recv.at[k], far(k))

    for j in range(AHEAD):
        weight_copy(0, j).start()
        weight_copy(1, j).start()

    barrier = pltpu.get_barrier_semaphore()
    for target in (sibling, across, far(1), far(2), far(3)):
        pl.semaphore_signal(barrier, inc=1, device_id=target, device_id_type=mesh_ids)

    @pl.when(jnp.logical_not(home))
    def _():
        pl.semaphore_signal(barrier, inc=1, device_id=far(0), device_id_type=mesh_ids)

    count = tokens.shape[0]
    grid = (quota, count)
    first = jnp.broadcast_to(pairs[0:1, :], grid)
    second = jnp.broadcast_to(pairs[1:2, :], grid)
    first_share = jnp.broadcast_to(shares[0:1, :], grid)
    second_share = jnp.broadcast_to(shares[1:2, :], grid)
    slot = lax.broadcasted_iota(jnp.int32, grid, 0)
    square = (count, count)
    earlier = (
        lax.broadcasted_iota(jnp.int32, square, 0) < lax.broadcasted_iota(jnp.int32, square, 1)
    )
    earlier = jnp.where(earlier, 1.0, 0.0).astype(jnp.bfloat16)

    def choose(k):
        expert = flip(e, k)
        limit = jnp.where(flags[expert] == 1, GROUP_QUOTA, quotas[expert])
        is_first = first == expert
        named = jnp.logical_or(is_first, second == expert)
        ones = jnp.where(named, 1.0, 0.0)
        rank = jnp.dot(ones.astype(jnp.bfloat16), earlier, preferred_element_type=jnp.float32)
        rank = rank.astype(jnp.int32)
        hit = jnp.logical_and(jnp.logical_and(named, rank == slot), slot < limit)
        picks[k] = jnp.where(hit, jnp.where(is_first, first_share, second_share), 0.0)
        chosen = jnp.where(hit, 1.0, 0.0).astype(jnp.bfloat16)
        return jnp.dot(chosen, tokens[...], preferred_element_type=jnp.float32).astype(
            jnp.bfloat16
        )

    nearest = choose(0)

    @pl.when(home)
    def _():
        rows[0, direct] = nearest
        pl.semaphore_wait(barrier, 5)

    @pl.when(jnp.logical_not(home))
    def _():
        packed[0] = nearest
        pl.semaphore_wait(barrier, 6)
        dispatch(0).start()

    for k in range(1, HOPS):
        packed[k] = choose(k)

    @pl.when(jnp.logical_not(home))
    def _():
        dispatch(0).wait_recv()

    forward(0).start()
    for k in range(1, HOPS):
        dispatch(k).start()
    forward(0).wait_recv()

    def body(s, carry):
        k = lax.div(s, PARTS)
        j = lax.rem(s, PARTS)

        @pl.when(s < STEPS)
        def _():
            @pl.when(jnp.logical_and(j == 0, k > 0))
            def _():
                forward(k).wait_recv()

            @pl.when(k == 0)
            def _():
                weight_copy(0, j).wait()
                weight_copy(1, j).wait()

                @pl.when(j + AHEAD < PARTS)
                def _():
                    weight_copy(0, j + AHEAD).start()
                    weight_copy(1, j + AHEAD).start()

            @pl.when(jnp.logical_and(s >= AHEAD, s < PARTS + AHEAD))
            def _():
                weight_copy(2, s - AHEAD).start()

            block = rows[k].reshape(2 * quota, rows.shape[3])
            gate = jnp.dot(block, gate_w[j], preferred_element_type=jnp.float32)
            keep[s, 0] = gate[:quota]
            part_out[s, 0] = gate[quota:].astype(jnp.bfloat16)
            up = jnp.dot(block, up_w[j], preferred_element_type=jnp.float32)
            keep[s, 1] = up[:quota]
            part_out[s, 1] = up[quota:].astype(jnp.bfloat16)
            part_copy(s).start()

            @pl.when(jnp.logical_and(j == PARTS // 2, k < HOPS - 1))
            def _():
                dispatch(k + 1).wait_recv()
                forward(k + 1).start()

        h = s - LAG_SUM

        @pl.when(jnp.logical_and(h >= 0, h < STEPS))
        def _():
            part_copy(h).wait_recv()
            gate = keep[h, 0] + part_in[h, 0].astype(jnp.float32)
            up = keep[h, 1] + part_in[h, 1].astype(jnp.float32)
            hid[h, 0] = (gate / (1.0 + jnp.exp(-gate)) * up).astype(jnp.bfloat16)
            hid_copy(h).start()

        q = s - LAG_SUM - LAG_DOWN

        @pl.when(q >= 0)
        def _():
            kq = lax.div(q, PARTS)
            jq = lax.rem(q, PARTS)
            hid_copy(q).wait_recv()

            @pl.when(kq == 0)
            def _():
                weight_copy(2, jq).wait()

            term = jnp.dot(
                hid[q].reshape(2 * quota, width), down_w[jq], preferred_element_type=jnp.float32
            ).reshape(2, quota, acc.shape[3])

            @pl.when(jq == 0)
            def _():
                acc[kq] = term

            @pl.when(jq > 0)
            def _():
                acc[kq] = acc[kq] + term

            @pl.when(jq == PARTS - 1)
            def _():
                core_copy(kq).start()
                core_copy(kq).wait_recv()
                total = (acc[kq, direct] + core_in[kq]).astype(jnp.bfloat16)
                stays = jnp.logical_and(home, kq == 0)

                @pl.when(stays)
                def _():
                    returned[0] = total

                @pl.when(jnp.logical_not(stays))
                def _():
                    back[kq] = total
                    back_copy(kq).start()

        return carry

    lax.fori_loop(0, STEPS + LAG_SUM + LAG_DOWN, body, 0)

    def mix(k):
        pick = picks[k]
        term = jnp.zeros(tokens.shape, jnp.float32)
        for _ in range(3):
            piece = pick.astype(jnp.bfloat16)
            term += lax.dot_general(
                piece, returned[k], (((0,), (0,)), ((), ())), preferred_element_type=jnp.float32
            )
            pick = pick - piece.astype(jnp.float32)
        return term

    @pl.when(jnp.logical_not(home))
    def _():
        back_copy(0).wait_recv()

    total = mix(0)
    for k in range(1, HOPS):
        back_copy(k).wait_recv()
        total += mix(k)
    out[...] = total.astype(out.dtype)

    def drain(s, carry):
        part_copy(s).wait_send()
        hid_copy(s).wait_send()
        return carry

    lax.fori_loop(0, STEPS, drain, 0)
    for k in range(HOPS):
        forward(k).wait_send()
        core_copy(k).wait_send()
        if k > 0:
            dispatch(k).wait_send()
            back_copy(k).wait_send()

    @pl.when(jnp.logical_not(home))
    def _():
        dispatch(0).wait_send()
        back_copy(0).wait_send()


def fused(
    incoming_activation_vectors,
    routed_specialist_pairs,
    routing_shares,
    popular_specialist_flags,
    group_quotas,
    gating_weight_stack,
    widen_weight_stack,
    contract_weight_stack,
):
    tok_rows, half_width = incoming_activation_vectors.shape
    width = gating_weight_stack.shape[1] // PARTS
    bf16, f32 = jnp.bfloat16, jnp.float32
    dma = pltpu.SemaphoreType.DMA
    quota = GROUP_QUOTA
    vmem = pl.BlockSpec(memory_space=pltpu.VMEM)
    smem = pl.BlockSpec(memory_space=pltpu.SMEM)
    return pl.pallas_call(
        layer_kernel,
        out_shape=jax.ShapeDtypeStruct((tok_rows, half_width), bf16),
        in_specs=[smem] * 2 + [vmem] * 3 + [pl.BlockSpec(memory_space=pl.ANY)] * 3,
        out_specs=vmem,
        scratch_shapes=[
            pltpu.VMEM((PARTS, half_width, width), bf16),
            pltpu.VMEM((PARTS, half_width, width), bf16),
            pltpu.VMEM((PARTS, width, half_width), bf16),
            pltpu.VMEM((HOPS, quota, half_width), bf16),
            pltpu.VMEM((HOPS, quota, tok_rows), f32),
            pltpu.VMEM((HOPS, quota, half_width), bf16),
            pltpu.VMEM((HOPS, 2, quota, half_width), bf16),
            pltpu.VMEM((STEPS, 2, quota, width), f32),
            pltpu.VMEM((STEPS, 2, quota, width), bf16),
            pltpu.VMEM((STEPS, 2, quota, width), bf16),
            pltpu.VMEM((STEPS, 2, quota, width), bf16),
            pltpu.VMEM((HOPS, 2, quota, half_width), f32),
            pltpu.VMEM((HOPS, quota, half_width), f32),
            pltpu.VMEM((HOPS, quota, half_width), bf16),
            dma((3, PARTS)),
            dma((HOPS,)),
            dma((HOPS,)),
            dma((HOPS,)),
            dma((HOPS,)),
            dma((STEPS,)),
            dma((STEPS,)),
            dma((STEPS,)),
            dma((STEPS,)),
            dma((HOPS,)),
            dma((HOPS,)),
            dma((HOPS,)),
            dma((HOPS,)),
        ],
        compiler_params=pltpu.CompilerParams(
            collective_id=0, has_side_effects=True, vmem_limit_bytes=60 * 1024 * 1024
        ),
        name="expert_layer",
    )(
        popular_specialist_flags,
        group_quotas,
        incoming_activation_vectors,
        routed_specialist_pairs.T,
        routing_shares.T,
        gating_weight_stack,
        widen_weight_stack,
        contract_weight_stack,
    )


def solution(mesh):
    shape = mesh.shape
    square = shape["dp"] == 2 and shape["tensor"] == 2 and shape["expert"] == EXPERTS
    local = fused if square else gathered
    placed = (
        P(("group", "expert", "dp"), "tensor"),
        P(("group", "expert", "dp"), None),
        P(("group", "expert", "dp"), None),
        P("group"),
        P("group"),
        P("dp", ("expert", "tensor")),
        P("dp", ("expert", "tensor")),
        P(("expert", "tensor"), "dp"),
    )
    return jax.shard_map(
        local,
        mesh=mesh,
        in_specs=placed,
        out_specs=P(("group", "expert", "dp"), "tensor"),
        check_vma=False,
    )
```

```python
import jax
import jax.numpy as jnp
from jax import lax
from jax.experimental import pallas as pl
from jax.experimental.pallas import tpu as pltpu
from jax.sharding import PartitionSpec as P

GROUP_QUOTA = 32
EXPERTS = 4


def gathered(
    incoming_activation_vectors,
    routed_specialist_pairs,
    routing_shares,
    popular_specialist_flags,
    group_quotas,
    gating_weight_stack,
    widen_weight_stack,
    contract_weight_stack,
):
    experts = popular_specialist_flags.shape[0]
    tok_rows = incoming_activation_vectors.shape[0]
    half_width = incoming_activation_vectors.shape[1]
    expert_count = lax.axis_size("expert")
    tensor_count = lax.axis_size("tensor")
    owners = expert_count // experts
    pair_ids = routed_specialist_pairs.reshape(-1)
    onehot = (pair_ids[:, None] == jnp.arange(experts, dtype=jnp.int32)[None, :]).astype(jnp.int32)
    slot_rank = jnp.sum((jnp.cumsum(onehot, axis=0) - onehot) * onehot, axis=1)
    quota_bound = jnp.where(popular_specialist_flags == 1, GROUP_QUOTA, group_quotas)
    kept_pair = slot_rank < jnp.sum(onehot * quota_bound[None, :], axis=1)
    target = jnp.where(kept_pair, pair_ids * GROUP_QUOTA + slot_rank, -1)
    select = (
        jnp.arange(experts * GROUP_QUOTA, dtype=jnp.int32)[:, None] == target[None, :]
    ).astype(jnp.bfloat16)
    select = select.reshape(experts * GROUP_QUOTA, tok_rows, 2).sum(axis=2)
    packed = jnp.dot(
        select, incoming_activation_vectors, preferred_element_type=jnp.float32
    ).astype(jnp.bfloat16)
    packed = packed.reshape(experts, GROUP_QUOTA, half_width)
    outgoing = jnp.repeat(packed, owners * tensor_count, axis=0)
    arrived = lax.all_to_all(
        outgoing, ("expert", "tensor"), split_axis=0, concat_axis=2, tiled=True
    )
    owner_rows = arrived.reshape(GROUP_QUOTA * expert_count, half_width * tensor_count)
    gate_part = jnp.dot(
        owner_rows,
        lax.all_gather(gating_weight_stack, "dp", axis=0, tiled=True),
        preferred_element_type=jnp.float32,
    )
    up_part = jnp.dot(
        owner_rows,
        lax.all_gather(widen_weight_stack, "dp", axis=0, tiled=True),
        preferred_element_type=jnp.float32,
    )
    hidden = (jax.nn.silu(gate_part) * up_part).astype(jnp.bfloat16)
    partial_value = jnp.dot(
        hidden,
        lax.all_gather(contract_weight_stack, "dp", axis=1, tiled=True),
        preferred_element_type=jnp.float32,
    )
    partial_value = partial_value.astype(jnp.bfloat16).reshape(
        1, GROUP_QUOTA, expert_count * tensor_count * half_width
    )
    returned = lax.all_to_all(
        partial_value, ("expert", "tensor"), split_axis=2, concat_axis=0, tiled=True
    )
    summed = (
        returned.astype(jnp.float32)
        .reshape(experts, owners * tensor_count, GROUP_QUOTA, half_width)
        .sum(axis=1)
    )
    summed = summed.reshape(experts * GROUP_QUOTA, half_width)
    pick_index = jnp.maximum(target, 0)
    weights_kept = jnp.where(kept_pair, routing_shares.reshape(-1), 0.0)
    picked = jnp.take(summed, pick_index, axis=0) * weights_kept[:, None]
    mixed = picked.reshape(tok_rows, 2, half_width).sum(axis=1)
    return mixed.astype(jnp.bfloat16)


HOPS = 4
PARTS = 4
STEPS = HOPS * PARTS
LAG_SUM = 3
LAG_DOWN = 3
AHEAD = 2


def flip(e, k):
    low = lax.rem(lax.rem(e, 2) + lax.div(k, 2), 2)
    high = lax.rem(lax.div(e, 2) + lax.div(k, 2) + lax.rem(k, 2), 2)
    return low + 2 * high


def layer_kernel(
    flags,
    quotas,
    tokens,
    pairs,
    shares,
    gate_hbm,
    up_hbm,
    down_hbm,
    out,
    gate_w,
    up_w,
    down_w,
    packed,
    picks,
    returned,
    rows,
    keep,
    part_out,
    part_in,
    hid,
    acc,
    core_in,
    back,
    w_sem,
    disp_send,
    disp_recv,
    fwd_send,
    fwd_recv,
    part_send,
    part_recv,
    hid_send,
    hid_recv,
    core_send,
    core_recv,
    back_send,
    back_recv,
):
    e = lax.axis_index("expert")
    d = lax.axis_index("dp")
    t = lax.axis_index("tensor")
    quota = packed.shape[1]
    width = gate_w.shape[2]
    mesh_ids = pl.DeviceIdType.MESH
    home = d == t
    direct = lax.rem(d + t, 2)

    def weight_copy(which, j):
        hbm, vmem = ((gate_hbm, gate_w), (up_hbm, up_w), (down_hbm, down_w))[which]
        start = pl.multiple_of(j * width, width)
        block = hbm.at[pl.ds(start, width), :] if which == 2 else hbm.at[:, pl.ds(start, width)]
        return pltpu.make_async_copy(block, vmem.at[j], w_sem.at[which, j])

    def far(k):
        return {"expert": flip(e, k), "dp": t, "tensor": d}

    sibling = {"expert": e, "dp": d, "tensor": 1 - t}
    across = {"expert": e, "dp": 1 - d, "tensor": t}

    def remote(src, dst, send, recv, target):
        return pltpu.make_async_remote_copy(
            src_ref=src,
            dst_ref=dst,
            send_sem=send,
            recv_sem=recv,
            device_id=target,
            device_id_type=mesh_ids,
        )

    def dispatch(k):
        return remote(
            packed.at[k], rows.at[k, direct], disp_send.at[k], disp_recv.at[k], far(k)
        )

    def forward(k):
        return remote(
            rows.at[k, direct], rows.at[k, direct], fwd_send.at[k], fwd_recv.at[k], sibling
        )

    def part_copy(s, i):
        return remote(
            part_out.at[s, i], part_in.at[s, i], part_send.at[s, i], part_recv.at[s, i], across
        )

    def hid_copy(s):
        return remote(hid.at[s, 0], hid.at[s, 1], hid_send.at[s], hid_recv.at[s], across)

    def core_copy(k):
        return remote(acc.at[k, 1 - direct], core_in.at[k], core_send.at[k], core_recv.at[k], sibling)

    def back_copy(k):
        return remote(back.at[k], returned.at[k], back_send.at[k], back_recv.at[k], far(k))

    for j in range(AHEAD):
        weight_copy(0, j).start()
        weight_copy(1, j).start()

    barrier = pltpu.get_barrier_semaphore()
    for target in (sibling, across, far(1), far(2), far(3)):
        pl.semaphore_signal(barrier, inc=1, device_id=target, device_id_type=mesh_ids)

    @pl.when(jnp.logical_not(home))
    def _():
        pl.semaphore_signal(barrier, inc=1, device_id=far(0), device_id_type=mesh_ids)

    count = tokens.shape[0]
    grid = (quota, count)
    first = jnp.broadcast_to(pairs[0:1, :], grid)
    second = jnp.broadcast_to(pairs[1:2, :], grid)
    first_share = jnp.broadcast_to(shares[0:1, :], grid)
    second_share = jnp.broadcast_to(shares[1:2, :], grid)
    slot = lax.broadcasted_iota(jnp.int32, grid, 0)
    square = (count, count)
    earlier = (
        lax.broadcasted_iota(jnp.int32, square, 0) < lax.broadcasted_iota(jnp.int32, square, 1)
    )
    earlier = jnp.where(earlier, 1.0, 0.0).astype(jnp.bfloat16)

    def choose(k):
        expert = flip(e, k)
        limit = jnp.where(flags[expert] == 1, GROUP_QUOTA, quotas[expert])
        is_first = first == expert
        named = jnp.logical_or(is_first, second == expert)
        ones = jnp.where(named, 1.0, 0.0)
        rank = jnp.dot(ones.astype(jnp.bfloat16), earlier, preferred_element_type=jnp.float32)
        rank = rank.astype(jnp.int32)
        hit = jnp.logical_and(jnp.logical_and(named, rank == slot), slot < limit)
        picks[k] = jnp.where(hit, jnp.where(is_first, first_share, second_share), 0.0)
        chosen = jnp.where(hit, 1.0, 0.0).astype(jnp.bfloat16)
        return jnp.dot(chosen, tokens[...], preferred_element_type=jnp.float32).astype(
            jnp.bfloat16
        )

    nearest = choose(0)

    @pl.when(home)
    def _():
        rows[0, direct] = nearest
        pl.semaphore_wait(barrier, 5)

    @pl.when(jnp.logical_not(home))
    def _():
        packed[0] = nearest
        pl.semaphore_wait(barrier, 6)
        dispatch(0).start()

    for k in range(1, HOPS):
        packed[k] = choose(k)

    @pl.when(jnp.logical_not(home))
    def _():
        dispatch(0).wait_recv()

    forward(0).start()
    for k in range(1, HOPS):
        dispatch(k).start()
    forward(0).wait_recv()

    def body(s, carry):
        k = lax.div(s, PARTS)
        j = lax.rem(s, PARTS)

        @pl.when(s < STEPS)
        def _():
            @pl.when(jnp.logical_and(j == 0, k > 0))
            def _():
                forward(k).wait_recv()

            @pl.when(k == 0)
            def _():
                weight_copy(0, j).wait()
                weight_copy(1, j).wait()

                @pl.when(j + AHEAD < PARTS)
                def _():
                    weight_copy(0, j + AHEAD).start()
                    weight_copy(1, j + AHEAD).start()

            @pl.when(jnp.logical_and(s >= AHEAD, s < PARTS + AHEAD))
            def _():
                weight_copy(2, s - AHEAD).start()

            block = rows[k].reshape(2 * quota, rows.shape[3])
            gate = jnp.dot(block, gate_w[j], preferred_element_type=jnp.float32)
            keep[s, 0] = gate[:quota]
            part_out[s, 0] = gate[quota:].astype(jnp.bfloat16)
            part_copy(s, 0).start()
            up = jnp.dot(block, up_w[j], preferred_element_type=jnp.float32)
            keep[s, 1] = up[:quota]
            part_out[s, 1] = up[quota:].astype(jnp.bfloat16)
            part_copy(s, 1).start()

            @pl.when(jnp.logical_and(j == PARTS // 2, k < HOPS - 1))
            def _():
                dispatch(k + 1).wait_recv()
                forward(k + 1).start()

        h = s - LAG_SUM

        @pl.when(jnp.logical_and(h >= 0, h < STEPS))
        def _():
            part_copy(h, 0).wait_recv()
            part_copy(h, 1).wait_recv()
            gate = keep[h, 0] + part_in[h, 0].astype(jnp.float32)
            up = keep[h, 1] + part_in[h, 1].astype(jnp.float32)
            hid[h, 0] = (gate / (1.0 + jnp.exp(-gate)) * up).astype(jnp.bfloat16)
            hid_copy(h).start()

        q = s - LAG_SUM - LAG_DOWN

        @pl.when(q >= 0)
        def _():
            kq = lax.div(q, PARTS)
            jq = lax.rem(q, PARTS)
            hid_copy(q).wait_recv()

            @pl.when(kq == 0)
            def _():
                weight_copy(2, jq).wait()

            term = jnp.dot(
                hid[q].reshape(2 * quota, width), down_w[jq], preferred_element_type=jnp.float32
            ).reshape(2, quota, acc.shape[3])

            @pl.when(jq == 0)
            def _():
                acc[kq] = term

            @pl.when(jq > 0)
            def _():
                acc[kq] = acc[kq] + term

            @pl.when(jq == PARTS - 1)
            def _():
                core_copy(kq).start()
                core_copy(kq).wait_recv()
                total = (acc[kq, direct] + core_in[kq]).astype(jnp.bfloat16)
                stays = jnp.logical_and(home, kq == 0)

                @pl.when(stays)
                def _():
                    returned[0] = total

                @pl.when(jnp.logical_not(stays))
                def _():
                    back[kq] = total
                    back_copy(kq).start()

        return carry

    lax.fori_loop(0, STEPS + LAG_SUM + LAG_DOWN, body, 0)

    def mix(k):
        pick = picks[k]
        term = jnp.zeros(tokens.shape, jnp.float32)
        for _ in range(3):
            piece = pick.astype(jnp.bfloat16)
            term += lax.dot_general(
                piece, returned[k], (((0,), (0,)), ((), ())), preferred_element_type=jnp.float32
            )
            pick = pick - piece.astype(jnp.float32)
        return term

    @pl.when(jnp.logical_not(home))
    def _():
        back_copy(0).wait_recv()

    total = mix(0)
    for k in range(1, HOPS):
        back_copy(k).wait_recv()
        total += mix(k)
    out[...] = total.astype(out.dtype)

    def drain(s, carry):
        part_copy(s, 0).wait_send()
        part_copy(s, 1).wait_send()
        hid_copy(s).wait_send()
        return carry

    lax.fori_loop(0, STEPS, drain, 0)
    for k in range(HOPS):
        forward(k).wait_send()
        core_copy(k).wait_send()
        if k > 0:
            dispatch(k).wait_send()
            back_copy(k).wait_send()

    @pl.when(jnp.logical_not(home))
    def _():
        dispatch(0).wait_send()
        back_copy(0).wait_send()


def fused(
    incoming_activation_vectors,
    routed_specialist_pairs,
    routing_shares,
    popular_specialist_flags,
    group_quotas,
    gating_weight_stack,
    widen_weight_stack,
    contract_weight_stack,
):
    tok_rows, half_width = incoming_activation_vectors.shape
    width = gating_weight_stack.shape[1] // PARTS
    bf16, f32 = jnp.bfloat16, jnp.float32
    dma = pltpu.SemaphoreType.DMA
    quota = GROUP_QUOTA
    vmem = pl.BlockSpec(memory_space=pltpu.VMEM)
    smem = pl.BlockSpec(memory_space=pltpu.SMEM)
    return pl.pallas_call(
        layer_kernel,
        out_shape=jax.ShapeDtypeStruct((tok_rows, half_width), bf16),
        in_specs=[smem] * 2 + [vmem] * 3 + [pl.BlockSpec(memory_space=pl.ANY)] * 3,
        out_specs=vmem,
        scratch_shapes=[
            pltpu.VMEM((PARTS, half_width, width), bf16),
            pltpu.VMEM((PARTS, half_width, width), bf16),
            pltpu.VMEM((PARTS, width, half_width), bf16),
            pltpu.VMEM((HOPS, quota, half_width), bf16),
            pltpu.VMEM((HOPS, quota, tok_rows), f32),
            pltpu.VMEM((HOPS, quota, half_width), bf16),
            pltpu.VMEM((HOPS, 2, quota, half_width), bf16),
            pltpu.VMEM((STEPS, 2, quota, width), f32),
            pltpu.VMEM((STEPS, 2, quota, width), bf16),
            pltpu.VMEM((STEPS, 2, quota, width), bf16),
            pltpu.VMEM((STEPS, 2, quota, width), bf16),
            pltpu.VMEM((HOPS, 2, quota, half_width), f32),
            pltpu.VMEM((HOPS, quota, half_width), f32),
            pltpu.VMEM((HOPS, quota, half_width), bf16),
            dma((3, PARTS)),
            dma((HOPS,)),
            dma((HOPS,)),
            dma((HOPS,)),
            dma((HOPS,)),
            dma((STEPS, 2)),
            dma((STEPS, 2)),
            dma((STEPS,)),
            dma((STEPS,)),
            dma((HOPS,)),
            dma((HOPS,)),
            dma((HOPS,)),
            dma((HOPS,)),
        ],
        compiler_params=pltpu.CompilerParams(
            collective_id=0, has_side_effects=True, vmem_limit_bytes=60 * 1024 * 1024
        ),
        name="expert_layer",
    )(
        popular_specialist_flags,
        group_quotas,
        incoming_activation_vectors,
        routed_specialist_pairs.T,
        routing_shares.T,
        gating_weight_stack,
        widen_weight_stack,
        contract_weight_stack,
    )


def solution(mesh):
    shape = mesh.shape
    square = shape["dp"] == 2 and shape["tensor"] == 2 and shape["expert"] == EXPERTS
    local = fused if square else gathered
    placed = (
        P(("group", "expert", "dp"), "tensor"),
        P(("group", "expert", "dp"), None),
        P(("group", "expert", "dp"), None),
        P("group"),
        P("group"),
        P("dp", ("expert", "tensor")),
        P("dp", ("expert", "tensor")),
        P(("expert", "tensor"), "dp"),
    )
    return jax.shard_map(
        local,
        mesh=mesh,
        in_specs=placed,
        out_specs=P(("group", "expert", "dp"), "tensor"),
        check_vma=False,
    )
```

```python
import jax
import jax.numpy as jnp
from jax import lax
from jax.experimental import pallas as pl
from jax.experimental.pallas import tpu as pltpu
from jax.sharding import PartitionSpec as P

GROUP_QUOTA = 32
EXPERTS = 4


def gathered(
    incoming_activation_vectors,
    routed_specialist_pairs,
    routing_shares,
    popular_specialist_flags,
    group_quotas,
    gating_weight_stack,
    widen_weight_stack,
    contract_weight_stack,
):
    experts = popular_specialist_flags.shape[0]
    tok_rows = incoming_activation_vectors.shape[0]
    half_width = incoming_activation_vectors.shape[1]
    expert_count = lax.axis_size("expert")
    tensor_count = lax.axis_size("tensor")
    owners = expert_count // experts
    pair_ids = routed_specialist_pairs.reshape(-1)
    onehot = (pair_ids[:, None] == jnp.arange(experts, dtype=jnp.int32)[None, :]).astype(jnp.int32)
    slot_rank = jnp.sum((jnp.cumsum(onehot, axis=0) - onehot) * onehot, axis=1)
    quota_bound = jnp.where(popular_specialist_flags == 1, GROUP_QUOTA, group_quotas)
    kept_pair = slot_rank < jnp.sum(onehot * quota_bound[None, :], axis=1)
    target = jnp.where(kept_pair, pair_ids * GROUP_QUOTA + slot_rank, -1)
    select = (
        jnp.arange(experts * GROUP_QUOTA, dtype=jnp.int32)[:, None] == target[None, :]
    ).astype(jnp.bfloat16)
    select = select.reshape(experts * GROUP_QUOTA, tok_rows, 2).sum(axis=2)
    packed = jnp.dot(
        select, incoming_activation_vectors, preferred_element_type=jnp.float32
    ).astype(jnp.bfloat16)
    packed = packed.reshape(experts, GROUP_QUOTA, half_width)
    outgoing = jnp.repeat(packed, owners * tensor_count, axis=0)
    arrived = lax.all_to_all(
        outgoing, ("expert", "tensor"), split_axis=0, concat_axis=2, tiled=True
    )
    owner_rows = arrived.reshape(GROUP_QUOTA * expert_count, half_width * tensor_count)
    gate_part = jnp.dot(
        owner_rows,
        lax.all_gather(gating_weight_stack, "dp", axis=0, tiled=True),
        preferred_element_type=jnp.float32,
    )
    up_part = jnp.dot(
        owner_rows,
        lax.all_gather(widen_weight_stack, "dp", axis=0, tiled=True),
        preferred_element_type=jnp.float32,
    )
    hidden = (jax.nn.silu(gate_part) * up_part).astype(jnp.bfloat16)
    partial_value = jnp.dot(
        hidden,
        lax.all_gather(contract_weight_stack, "dp", axis=1, tiled=True),
        preferred_element_type=jnp.float32,
    )
    partial_value = partial_value.astype(jnp.bfloat16).reshape(
        1, GROUP_QUOTA, expert_count * tensor_count * half_width
    )
    returned = lax.all_to_all(
        partial_value, ("expert", "tensor"), split_axis=2, concat_axis=0, tiled=True
    )
    summed = (
        returned.astype(jnp.float32)
        .reshape(experts, owners * tensor_count, GROUP_QUOTA, half_width)
        .sum(axis=1)
    )
    summed = summed.reshape(experts * GROUP_QUOTA, half_width)
    pick_index = jnp.maximum(target, 0)
    weights_kept = jnp.where(kept_pair, routing_shares.reshape(-1), 0.0)
    picked = jnp.take(summed, pick_index, axis=0) * weights_kept[:, None]
    mixed = picked.reshape(tok_rows, 2, half_width).sum(axis=1)
    return mixed.astype(jnp.bfloat16)


HOPS = 4
PARTS = 4
STEPS = HOPS * PARTS
LAG_SUM = 3
LAG_DOWN = 3
AHEAD = 2


def flip(e, k):
    low = lax.rem(lax.rem(e, 2) + lax.div(k, 2), 2)
    high = lax.rem(lax.div(e, 2) + lax.div(k, 2) + lax.rem(k, 2), 2)
    return low + 2 * high


def layer_kernel(
    flags,
    quotas,
    tokens,
    pairs,
    shares,
    gate_hbm,
    up_hbm,
    down_hbm,
    out,
    gate_w,
    up_w,
    down_w,
    own_pairs,
    src_pairs,
    src_tokens,
    packed,
    picks,
    returned,
    rows,
    keep,
    part_out,
    part_in,
    hid,
    acc,
    core_in,
    back,
    w_sem,
    swap_send,
    swap_recv,
    disp_send,
    disp_recv,
    fwd_send,
    fwd_recv,
    part_send,
    part_recv,
    hid_send,
    hid_recv,
    core_send,
    core_recv,
    back_send,
    back_recv,
):
    e = lax.axis_index("expert")
    d = lax.axis_index("dp")
    t = lax.axis_index("tensor")
    quota = packed.shape[1]
    width = gate_w.shape[2]
    mesh_ids = pl.DeviceIdType.MESH
    home = d == t
    direct = lax.rem(d + t, 2)

    def weight_copy(which, j):
        hbm, vmem = ((gate_hbm, gate_w), (up_hbm, up_w), (down_hbm, down_w))[which]
        start = pl.multiple_of(j * width, width)
        block = hbm.at[pl.ds(start, width), :] if which == 2 else hbm.at[:, pl.ds(start, width)]
        return pltpu.make_async_copy(block, vmem.at[j], w_sem.at[which, j])

    def far(k):
        return {"expert": flip(e, k), "dp": t, "tensor": d}

    def along(k):
        return {"expert": flip(e, k), "dp": d, "tensor": t}

    sibling = {"expert": e, "dp": d, "tensor": 1 - t}
    across = {"expert": e, "dp": 1 - d, "tensor": t}

    def remote(src, dst, send, recv, target):
        return pltpu.make_async_remote_copy(
            src_ref=src,
            dst_ref=dst,
            send_sem=send,
            recv_sem=recv,
            device_id=target,
            device_id_type=mesh_ids,
        )

    def swap(i):
        src, dst = ((own_pairs, src_pairs), (tokens, src_tokens))[i]
        return remote(src, dst, swap_send.at[i], swap_recv.at[i], far(0))

    def dispatch(k):
        return remote(
            packed.at[k], rows.at[k, direct], disp_send.at[k], disp_recv.at[k], along(k)
        )

    def forward(k):
        return remote(
            rows.at[k, direct], rows.at[k, direct], fwd_send.at[k], fwd_recv.at[k], sibling
        )

    def part_copy(s, i):
        return remote(
            part_out.at[s, i], part_in.at[s, i], part_send.at[s, i], part_recv.at[s, i], across
        )

    def hid_copy(s):
        return remote(hid.at[s, 0], hid.at[s, 1], hid_send.at[s], hid_recv.at[s], across)

    def core_copy(k):
        return remote(acc.at[k, 1 - direct], core_in.at[k], core_send.at[k], core_recv.at[k], sibling)

    def back_copy(k):
        return remote(back.at[k], returned.at[k], back_send.at[k], back_recv.at[k], far(k))

    for j in range(AHEAD):
        weight_copy(0, j).start()
        weight_copy(1, j).start()

    barrier = pltpu.get_barrier_semaphore()
    for target in (sibling, across, far(1), far(2), far(3)):
        pl.semaphore_signal(barrier, inc=1, device_id=target, device_id_type=mesh_ids)

    @pl.when(jnp.logical_not(home))
    def _():
        for target in (far(0), along(1), along(2), along(3)):
            pl.semaphore_signal(barrier, inc=1, device_id=target, device_id_type=mesh_ids)

    count = tokens.shape[0]
    grid = (quota, count)
    slot = lax.broadcasted_iota(jnp.int32, grid, 0)
    square = (count, count)
    earlier = (
        lax.broadcasted_iota(jnp.int32, square, 0) < lax.broadcasted_iota(jnp.int32, square, 1)
    )
    earlier = jnp.where(earlier, 1.0, 0.0).astype(jnp.bfloat16)

    own_pairs[...] = jnp.zeros(own_pairs.shape, jnp.int32)
    own_pairs[0:2, 0:count] = pairs[...]

    @pl.when(home)
    def _():
        src_pairs[...] = own_pairs[...]
        src_tokens[...] = tokens[...]
        pl.semaphore_wait(barrier, 5)

    @pl.when(jnp.logical_not(home))
    def _():
        pl.semaphore_wait(barrier, 9)
        swap(0).start()
        swap(1).start()

    def slots_of(k, named_by):
        expert = flip(e, k)
        limit = jnp.where(flags[expert] == 1, GROUP_QUOTA, quotas[expert])
        is_first = jnp.broadcast_to(named_by[0:1, 0:count], grid) == expert
        is_second = jnp.broadcast_to(named_by[1:2, 0:count], grid) == expert
        named = jnp.logical_or(is_first, is_second)
        ones = jnp.where(named, 1.0, 0.0)
        rank = jnp.dot(ones.astype(jnp.bfloat16), earlier, preferred_element_type=jnp.float32)
        rank = rank.astype(jnp.int32)
        return jnp.logical_and(jnp.logical_and(named, rank == slot), slot < limit), is_first

    def choose(k):
        hit, _ = slots_of(k, src_pairs)
        chosen = jnp.where(hit, 1.0, 0.0).astype(jnp.bfloat16)
        return jnp.dot(chosen, src_tokens[...], preferred_element_type=jnp.float32).astype(
            jnp.bfloat16
        )

    first_share = jnp.broadcast_to(shares[0:1, :], grid)
    second_share = jnp.broadcast_to(shares[1:2, :], grid)
    for k in range(HOPS):
        hit, is_first = slots_of(k, own_pairs)
        picks[k] = jnp.where(hit, jnp.where(is_first, first_share, second_share), 0.0)

    @pl.when(jnp.logical_not(home))
    def _():
        swap(0).wait_recv()
        swap(1).wait_recv()

    rows[0, direct] = choose(0)
    forward(0).start()
    for k in range(1, HOPS):
        packed[k] = choose(k)
        dispatch(k).start()
    forward(0).wait_recv()

    def body(s, carry):
        k = lax.div(s, PARTS)
        j = lax.rem(s, PARTS)

        @pl.when(s < STEPS)
        def _():
            @pl.when(jnp.logical_and(j == 0, k > 0))
            def _():
                forward(k).wait_recv()

            @pl.when(k == 0)
            def _():
                weight_copy(0, j).wait()
                weight_copy(1, j).wait()

                @pl.when(j + AHEAD < PARTS)
                def _():
                    weight_copy(0, j + AHEAD).start()
                    weight_copy(1, j + AHEAD).start()

            @pl.when(jnp.logical_and(s >= AHEAD, s < PARTS + AHEAD))
            def _():
                weight_copy(2, s - AHEAD).start()

            block = rows[k].reshape(2 * quota, rows.shape[3])
            gate = jnp.dot(block, gate_w[j], preferred_element_type=jnp.float32)
            keep[s, 0] = gate[:quota]
            part_out[s, 0] = gate[quota:].astype(jnp.bfloat16)
            part_copy(s, 0).start()
            up = jnp.dot(block, up_w[j], preferred_element_type=jnp.float32)
            keep[s, 1] = up[:quota]
            part_out[s, 1] = up[quota:].astype(jnp.bfloat16)
            part_copy(s, 1).start()

            @pl.when(jnp.logical_and(j == PARTS // 2, k < HOPS - 1))
            def _():
                dispatch(k + 1).wait_recv()
                forward(k + 1).start()

        h = s - LAG_SUM

        @pl.when(jnp.logical_and(h >= 0, h < STEPS))
        def _():
            part_copy(h, 0).wait_recv()
            part_copy(h, 1).wait_recv()
            gate = keep[h, 0] + part_in[h, 0].astype(jnp.float32)
            up = keep[h, 1] + part_in[h, 1].astype(jnp.float32)
            hid[h, 0] = (gate / (1.0 + jnp.exp(-gate)) * up).astype(jnp.bfloat16)
            hid_copy(h).start()

        q = s - LAG_SUM - LAG_DOWN

        @pl.when(q >= 0)
        def _():
            kq = lax.div(q, PARTS)
            jq = lax.rem(q, PARTS)
            hid_copy(q).wait_recv()

            @pl.when(kq == 0)
            def _():
                weight_copy(2, jq).wait()

            term = jnp.dot(
                hid[q].reshape(2 * quota, width), down_w[jq], preferred_element_type=jnp.float32
            ).reshape(2, quota, acc.shape[3])

            @pl.when(jq == 0)
            def _():
                acc[kq] = term

            @pl.when(jq > 0)
            def _():
                acc[kq] = acc[kq] + term

            @pl.when(jq == PARTS - 1)
            def _():
                core_copy(kq).start()
                core_copy(kq).wait_recv()
                total = (acc[kq, direct] + core_in[kq]).astype(jnp.bfloat16)
                stays = jnp.logical_and(home, kq == 0)

                @pl.when(stays)
                def _():
                    returned[0] = total

                @pl.when(jnp.logical_not(stays))
                def _():
                    back[kq] = total
                    back_copy(kq).start()

        return carry

    lax.fori_loop(0, STEPS + LAG_SUM + LAG_DOWN, body, 0)

    def mix(k):
        pick = picks[k]
        term = jnp.zeros(tokens.shape, jnp.float32)
        for _ in range(3):
            piece = pick.astype(jnp.bfloat16)
            term += lax.dot_general(
                piece, returned[k], (((0,), (0,)), ((), ())), preferred_element_type=jnp.float32
            )
            pick = pick - piece.astype(jnp.float32)
        return term

    @pl.when(jnp.logical_not(home))
    def _():
        back_copy(0).wait_recv()

    total = mix(0)
    for k in range(1, HOPS):
        back_copy(k).wait_recv()
        total += mix(k)
    out[...] = total.astype(out.dtype)

    def drain(s, carry):
        part_copy(s, 0).wait_send()
        part_copy(s, 1).wait_send()
        hid_copy(s).wait_send()
        return carry

    lax.fori_loop(0, STEPS, drain, 0)
    for k in range(HOPS):
        forward(k).wait_send()
        core_copy(k).wait_send()
        if k > 0:
            dispatch(k).wait_send()
            back_copy(k).wait_send()

    @pl.when(jnp.logical_not(home))
    def _():
        swap(0).wait_send()
        swap(1).wait_send()
        back_copy(0).wait_send()


def fused(
    incoming_activation_vectors,
    routed_specialist_pairs,
    routing_shares,
    popular_specialist_flags,
    group_quotas,
    gating_weight_stack,
    widen_weight_stack,
    contract_weight_stack,
):
    tok_rows, half_width = incoming_activation_vectors.shape
    width = gating_weight_stack.shape[1] // PARTS
    bf16, f32 = jnp.bfloat16, jnp.float32
    dma = pltpu.SemaphoreType.DMA
    quota = GROUP_QUOTA
    vmem = pl.BlockSpec(memory_space=pltpu.VMEM)
    smem = pl.BlockSpec(memory_space=pltpu.SMEM)
    return pl.pallas_call(
        layer_kernel,
        out_shape=jax.ShapeDtypeStruct((tok_rows, half_width), bf16),
        in_specs=[smem] * 2 + [vmem] * 3 + [pl.BlockSpec(memory_space=pl.ANY)] * 3,
        out_specs=vmem,
        scratch_shapes=[
            pltpu.VMEM((PARTS, half_width, width), bf16),
            pltpu.VMEM((PARTS, half_width, width), bf16),
            pltpu.VMEM((PARTS, width, half_width), bf16),
            pltpu.VMEM((8, 128), jnp.int32),
            pltpu.VMEM((8, 128), jnp.int32),
            pltpu.VMEM((tok_rows, half_width), bf16),
            pltpu.VMEM((HOPS, quota, half_width), bf16),
            pltpu.VMEM((HOPS, quota, tok_rows), f32),
            pltpu.VMEM((HOPS, quota, half_width), bf16),
            pltpu.VMEM((HOPS, 2, quota, half_width), bf16),
            pltpu.VMEM((STEPS, 2, quota, width), f32),
            pltpu.VMEM((STEPS, 2, quota, width), bf16),
            pltpu.VMEM((STEPS, 2, quota, width), bf16),
            pltpu.VMEM((STEPS, 2, quota, width), bf16),
            pltpu.VMEM((HOPS, 2, quota, half_width), f32),
            pltpu.VMEM((HOPS, quota, half_width), f32),
            pltpu.VMEM((HOPS, quota, half_width), bf16),
            dma((3, PARTS)),
            dma((2,)),
            dma((2,)),
            dma((HOPS,)),
            dma((HOPS,)),
            dma((HOPS,)),
            dma((HOPS,)),
            dma((STEPS, 2)),
            dma((STEPS, 2)),
            dma((STEPS,)),
            dma((STEPS,)),
            dma((HOPS,)),
            dma((HOPS,)),
            dma((HOPS,)),
            dma((HOPS,)),
        ],
        compiler_params=pltpu.CompilerParams(
            collective_id=0, has_side_effects=True, vmem_limit_bytes=60 * 1024 * 1024
        ),
        name="expert_layer",
    )(
        popular_specialist_flags,
        group_quotas,
        incoming_activation_vectors,
        routed_specialist_pairs.T,
        routing_shares.T,
        gating_weight_stack,
        widen_weight_stack,
        contract_weight_stack,
    )


def solution(mesh):
    shape = mesh.shape
    square = shape["dp"] == 2 and shape["tensor"] == 2 and shape["expert"] == EXPERTS
    local = fused if square else gathered
    placed = (
        P(("group", "expert", "dp"), "tensor"),
        P(("group", "expert", "dp"), None),
        P(("group", "expert", "dp"), None),
        P("group"),
        P("group"),
        P("dp", ("expert", "tensor")),
        P("dp", ("expert", "tensor")),
        P(("expert", "tensor"), "dp"),
    )
    return jax.shard_map(
        local,
        mesh=mesh,
        in_specs=placed,
        out_specs=P(("group", "expert", "dp"), "tensor"),
        check_vma=False,
    )
```
